256 devices in a mesh: row: 8 (over x, y_hi), col: 32 (over z, y_lo, core).
Axes of the slice: x: 4, y: 4 (y_hi: 2, y_lo: 2; y = y_hi * 2 + y_lo), z: 8, core: 2. Of those that a mesh axis runs over, the one named last changes fastest.
Arguments:
- matrix: float32 [3, 8, 128, 32, 32, 128], P(None, 'row', None, None, 'col'), may hold values from -6 to 6
- factors: float32 [10, 512, 512], P(None, None, 'col'), as said below
- starts: int32 [10], replicated, may hold values from 0 to 2560, as said below
Outputs:
- updated: float32 [3, 8, 128, 32, 32, 128], P(None, 'row', None, None, 'col')
The draws below stay inside these ranges and needn't reach their ends.
Inputs may be any that keep to these rules, and one draw needn't show every extreme that they name: starts[w] = starts[0] + 256 * w, and starts[0] is a multiple of 128. Each factors[w] is orthogonal.
All inputs are finite; a program needn't handle non-finite values.
Results may differ from the reference program's by a relative error of at most 0.0001.
Values sent between devices are 32-bit elements; how exact they have to be, the bound alone decides.
A program may use at most 128 MiB of HBM per device.

```python
import jax
import jax.numpy as jnp
from jax import lax

ORDER = 131072
ROWS = 3072
NB = 128
WIN = 512
SHIFT = 256
WINS = 10
RCYC = 3
CCYC = 32
N_ROW = 8
N_COL = 32


def draw_factors(key, part):
    normal_draw = jax.random.normal(key, (WINS, WIN, WIN), jnp.float32)
    ortho_part, upper_part = jnp.linalg.qr(normal_draw)
    return ortho_part.astype(jnp.float32)


def draw_starts(key, part):
    choices_count = (ROWS - (WIN + SHIFT * (WINS - 1))) // NB + 1
    base_tile = jax.random.randint(jax.random.fold_in(key, 7), (), 0, choices_count, dtype=jnp.int32)
    return (base_tile * NB + SHIFT * jnp.arange(WINS, dtype=jnp.int32)).astype(jnp.int32)


def steps_of(rng, extent, pieces, smallest, top_value):
    def one(dim, blocks):
        steps = jax.random.uniform(jax.random.fold_in(jax.random.fold_in(rng, 6), dim), (blocks,), jnp.float32, smallest / len(pieces), top_value / len(pieces))
        return jnp.repeat(jnp.exp(steps), extent[dim] // blocks).reshape((-1,) + (1,) * (len(extent) - dim - 1))

    gain = one(*pieces[0])
    for cut in pieces[1:]:
        gain = gain * one(*cut)
    return gain


def gaussian(key, shape, deviation, bound, split=(), kind=jnp.bfloat16):
    values = deviation * jax.random.normal(key, shape, jnp.float32)
    if split:
        values = values * steps_of(key, shape, split, -0.22, 0.18)
    return jnp.clip(values, -bound, bound).astype(kind)


def setup_inputs(seed: int = 0) -> dict:
    seeds = jax.random.split(jax.random.key(seed), 4)
    matrix = gaussian(seeds[0], (RCYC, N_ROW, NB, CCYC, N_COL, NB), 1.0, 6.0, ((1, 8), (4, 32)), jnp.float32)
    factors = draw_factors(jax.random.fold_in(seeds[3], 71), 0)
    starts = draw_starts(jax.random.fold_in(seeds[3], 71), 0)
    return dict(matrix=matrix, factors=factors, starts=starts)


def reference(matrix, factors, starts):
    matrix_rows = matrix.reshape(ROWS, ORDER)
    for window in range(WINS):
        offset_row = starts[window].astype(jnp.int32)
        window_rows = lax.dynamic_slice_in_dim(matrix_rows, offset_row, WIN, 0)
        result_rows = jnp.dot(factors[window].T.astype(jnp.float32), window_rows.astype(jnp.float32), precision=lax.Precision.HIGHEST, preferred_element_type=jnp.float32)
        matrix_rows = lax.dynamic_update_slice_in_dim(matrix_rows, result_rows, offset_row, 0)
    for window in range(WINS):
        offset_col = starts[window].astype(jnp.int32)
        window_cols = lax.dynamic_slice_in_dim(matrix_rows, offset_col, WIN, 1)
        result_cols = jnp.dot(window_cols.astype(jnp.float32), factors[window].astype(jnp.float32), precision=lax.Precision.HIGHEST, preferred_element_type=jnp.float32)
        matrix_rows = lax.dynamic_update_slice_in_dim(matrix_rows, result_cols, offset_col, 1)
    return matrix_rows.reshape(matrix.shape)
```

```python
import functools

import jax
import jax.numpy as jnp
from jax import lax
from jax.experimental import pallas as pl
from jax.experimental.pallas import tpu as pltpu
from jax.sharding import PartitionSpec as P

MESH = pl.DeviceIdType.MESH
NB = 128
WIN = 512
WINS = 10
SPAN = 22
GROUPS = 5
ROWP = 8
COLP = 32
HELD = 4
DEPTH = 3
PEERS = ((0, 1), (1, 0), (2, 1), (3, 0), (1, 1), (2, 0), (3, 1))


def when(condition, action):
    if isinstance(condition, bool):
        if condition:
            action()
    else:
        pl.when(condition)(action)


def both(*conditions):
    result = True
    for condition in conditions:
        if condition is True:
            continue
        if condition is False:
            return False
        result = condition if result is True else jnp.logical_and(result, condition)
    return result


def split(value):
    high = value.astype(jnp.bfloat16)
    low = (value - high.astype(jnp.float32)).astype(jnp.bfloat16)
    return high, low


def dot(a, b):
    return jnp.dot(a, b, preferred_element_type=jnp.float32)


def dot_t(a, b):
    return lax.dot_general(a, b, (((1,), (1,)), ((), ())), preferred_element_type=jnp.float32)


def kernel(first, m, qt, o, band, qf, qh, ql, xh, xl, rbuf, cbuf,
           out_s, out_r, back_s, back_r, own_s, bown_s, rest_s,
           loc_s, y_s, y_r, zp_s, zp_r, zm_s, zm_r, c_s, c_r,
           rr_s, rr_r, rt_s, rt_r, c0_s, c0_r, cb_s, cb_r):
    p = lax.axis_index("row")
    q = lax.axis_index("col")
    x, yh = p // 2, p % 2
    z, yl, core = q // 4, (q // 2) % 2, q % 2

    dsts = [((x + dx) % 4) * 2 + (yh + dy) % 2 for dx, dy in PEERS]
    srcs = [((x + 4 - dx) % 4) * 2 + (yh + dy) % 2 for dx, dy in PEERS]

    def remote(src, dst, ss, rs, row, col):
        return pltpu.make_async_remote_copy(
            src, dst, ss, rs, device_id={"row": row, "col": col}, device_id_type=MESH
        )

    def local(src, dst, s):
        return pltpu.make_async_copy(src, dst, s)

    def in_band(r, s):
        tile = r * 8 + s
        if isinstance(tile, int):
            return first <= tile < first + SPAN
        if isinstance(r, int):
            return True if r == 1 else tile >= first if r == 0 else tile < first + SPAN
        return jnp.logical_and(tile >= first, tile < first + SPAN)

    def rows(tile):
        return pl.ds(pl.multiple_of(tile * NB, NB), NB)

    barrier = pltpu.get_barrier_semaphore()
    for d in dsts:
        pl.semaphore_signal(barrier, inc=1, device_id={"row": d, "col": q}, device_id_type=MESH)

    @pl.loop(1, COLP)
    def _(u):
        pl.semaphore_signal(
            barrier, inc=1, device_id={"row": p, "col": (q + u) % COLP}, device_id_type=MESH
        )

    pl.semaphore_wait(barrier, len(PEERS) + COLP - 1)

    mine = jnp.logical_and(q >= first, q < first + SPAN)

    def col_in(s):
        return jnp.logical_and(s >= first, s < first + SPAN)

    def right_send(u):
        to = (q + u) % COLP
        return remote(
            m.at[:, pl.ds(4 * to, 4), 0, 0], rbuf.at[q, pl.ds(0, 3)], rr_s.at[1], rr_r.at[0], p, to
        )

    def right_own():
        return local(m.at[:, pl.ds(4 * q, 4), 0, 0], rbuf.at[q, pl.ds(0, 3)], rr_s.at[0])

    def right_received(count):
        ref = rbuf.at[pl.ds(0, count), pl.ds(0, 3)]
        remote(ref, ref, rr_s.at[1], rr_r.at[0], dsts[0], q).wait_recv()

    def right_back(u):
        to = (q + u) % COLP
        return remote(
            rbuf.at[to, pl.ds(0, 3)], cbuf.at[:, pl.ds(4 * q, 4), 0], rt_s.at[1], rt_r.at[0], p, to
        )

    def right_back_own():
        return local(rbuf.at[q, pl.ds(0, 3)], cbuf.at[:, pl.ds(4 * q, 4), 0], rt_s.at[0])

    def cols_plain():
        return local(m.at[:, :, 0], cbuf, rt_s.at[0])

    def pair(g, zz, which, n=2, at=0):
        return qf.at[pl.ds(2 * g + at, n), zz, which]

    def own_share(g):
        return local(qt.at[pl.ds(2 * g, 2)], qf.at[pl.ds(2 * g, 2), z, core, yl], loc_s.at[g])

    def y_share(g):
        return remote(
            qt.at[pl.ds(2 * g, 2)], qf.at[pl.ds(2 * g, 2), z, core, yl], y_s.at[0], y_r.at[g],
            p, z * 4 + (1 - yl) * 2 + core,
        )

    def plus(g, j, zz):
        ref = pair(g, zz, core) if j < 3 else pair(g, zz, core, 1, 0)
        return remote(ref, ref, zp_s.at[0], zp_r.at[g, j], p, ((z + 1) % 8) * 4 + yl * 2 + core)

    def minus(g, j, zz):
        ref = pair(g, zz, core) if j < 3 else pair(g, zz, core, 1, 1)
        return remote(ref, ref, zm_s.at[0], zm_r.at[g, j], p, ((z + 7) % 8) * 4 + yl * 2 + core)

    def across(g, b, zz):
        ref = pair(g, zz, core)
        return remote(ref, ref, c_s.at[0], c_r.at[g], p, z * 4 + yl * 2 + 1 - core)

    block_z = [z, (z + 7) % 8, (z + 6) % 8, (z + 5) % 8, (z + 1) % 8, (z + 2) % 8, (z + 3) % 8, (z + 4) % 8]

    def out_copy(r, h, k):
        d = dsts[k]
        return remote(
            m.at[r, :, 4 * d + h, 0], band.at[h, rows(r * 8 + p)], out_s.at[r, h], out_r.at[r], d, q
        )

    def own_copy(r, h):
        return local(m.at[r, :, 4 * p + h, 0], band.at[h, rows(r * 8 + p)], own_s.at[r])

    def held(h, who):
        return jnp.logical_not(jnp.logical_and(h == 0, who == 0))

    def out_batch(i):
        r, h = i // HELD, i % HELD

        @pl.when(i >= DEPTH)
        def _():
            out_sent(i - DEPTH)

        for k, d in enumerate(dsts):
            when(both(in_band(r, p), held(h, d)), lambda k=k: out_copy(r, h, k).start())
        when(both(in_band(r, p), held(h, p)), lambda: own_copy(r, h).start())

    def tiles_ref(slots, count):
        return band.at[pl.ds(0, slots), pl.ds(0, count * NB)]

    def await_sent(slots, count, sem):
        ref = tiles_ref(slots, count)
        remote(ref, ref, sem, out_r.at[0], dsts[0], q).wait_send()

    def await_received(slots, count, sem):
        ref = tiles_ref(slots, count)
        remote(ref, ref, out_s.at[0, 0], sem, dsts[0], q).wait_recv()

    def per_peer(r, action):
        valid = sum(in_band(r, s) for s in range(8))
        for slots, which in ((HELD, p != 0), (HELD - 1, p == 0)):
            when(both(which, in_band(r, p)), lambda slots=slots: action(slots, valid - 1))
            if r != 1:
                when(
                    both(which, jnp.logical_not(in_band(r, p))),
                    lambda slots=slots: action(slots, valid),
                )

    def own_wait(r, sem):
        for slots, which in ((HELD, p != 0), (HELD - 1, p == 0)):
            ref = tiles_ref(slots, 1)
            when(both(which, in_band(r, p)), lambda ref=ref: local(ref, ref, sem).wait())

    def out_wait(r):
        per_peer(r, lambda slots, count: await_received(slots, count, out_r.at[r]))
        own_wait(r, own_s.at[r])

    def out_sent(i):
        r, h = i // HELD, i % HELD
        fewer = jnp.logical_and(h == 0, p != 0)
        when(both(in_band(r, p), fewer), lambda: await_sent(1, 6, out_s.at[r, h]))
        when(both(in_band(r, p), jnp.logical_not(fewer)), lambda: await_sent(1, 7, out_s.at[r, h]))

    def back_copy(r, h, k):
        d = dsts[k]
        return remote(
            band.at[h, rows(r * 8 + d)], o.at[r, :, 4 * p + h, 0], back_s.at[r], back_r.at[r], d, q
        )

    def back_own(r, h):
        return local(band.at[h, rows(r * 8 + p)], o.at[r, :, 4 * p + h, 0], bown_s.at[r])

    def back_send(r):
        @pl.loop(0, HELD)
        def _(h):
            for k, d in enumerate(dsts):
                when(both(in_band(r, d), held(h, p)), lambda k=k: back_copy(r, h, k).start())
            when(both(in_band(r, p), held(h, p)), lambda: back_own(r, h).start())

    def back_wait(r):
        per_peer(r, lambda slots, count: await_sent(slots, count, back_s.at[r]))
        own_wait(r, bown_s.at[r])
        when(both(in_band(r, p), p == 0), lambda: await_received(4, 7, back_r.at[r]))
        when(both(in_band(r, p), p != 0), lambda: await_received(3, 9, back_r.at[r]))

    def rest_copy(r):
        return local(m.at[r, :, pl.ds(1, 31)], o.at[r, :, pl.ds(1, 31)], rest_s.at[r, 0])

    def rest_first(r):
        return local(cbuf.at[r], o.at[r, :, 0], rest_s.at[r, 1])

    def first_out(r):
        return remote(cbuf.at[r, :, 0], band.at[HELD, rows(r * 8 + p)], c0_s.at[r], c0_r.at[r, p], 0, q)

    def first_in(r, s):
        return remote(cbuf.at[r, :, 0], band.at[HELD, rows(r * 8 + s)], c0_s.at[r], c0_r.at[r, s], 0, q)

    def first_own(r):
        return local(cbuf.at[r, :, 0], band.at[HELD, rows(r * 8)], c0_s.at[r])

    def first_back(r, s):
        return remote(band.at[HELD, rows(r * 8 + s)], o.at[r, :, 0, 0], cb_s.at[r, s], cb_r.at[r], s, q)

    def first_back_own(r):
        return local(band.at[HELD, rows(r * 8)], o.at[r, :, 0, 0], cb_s.at[r, 0])

    def convert(w):
        @pl.loop(0, 8)
        def _(zz):
            for a in range(2):
                for b in range(2):
                    at = pl.ds(pl.multiple_of(zz * 64 + b * 32 + a * 16, 16), 16)
                    high, low = split(qf[w, zz, a, b])
                    qh[w, at, :] = high
                    ql[w, at, :] = low

    def left_window(w, h, n):
        base = (first + 2 * w) * NB
        for i in range(n):
            high, low = split(band[h + i, pl.ds(pl.multiple_of(base, NB), WIN), :])
            xh[:, i * NB:(i + 1) * NB] = high
            xl[:, i * NB:(i + 1) * NB] = low
        xhv, xlv = xh[:, : n * NB], xl[:, : n * NB]

        @pl.loop(0, 2)
        def _(part):
            at = pl.ds(pl.multiple_of(part * 256, 256), 256)
            qhv, qlv = qh[w, at, :], ql[w, at, :]
            y = dot(qhv, xhv) + dot(qhv, xlv) + dot(qlv, xhv)
            to = pl.ds(pl.multiple_of(base + part * 256, NB), 256)
            for i in range(n):
                band[h + i, to, :] = y[:, i * NB:(i + 1) * NB]

    flat = rbuf.reshape(24 * 16, NB)

    def right_window(w):
        ats = [pl.ds(pl.multiple_of((first + 2 * w + j) * 16, 16), 16) for j in range(4)]
        value = jnp.concatenate([flat[at, :] for at in ats], axis=1)
        high, low = split(value)
        qhv, qlv = qh[w], ql[w]
        y = dot_t(high, qhv) + dot_t(low, qhv) + dot_t(high, qlv)
        for j, at in enumerate(ats):
            flat[at, :] = y[:, j * NB:(j + 1) * NB]

    when(mine, lambda: right_own().start())

    @pl.when(mine)
    def _():
        @pl.loop(1, COLP)
        def _(u):
            right_send(u).start()

    when(jnp.logical_not(mine), lambda: cols_plain().start())
    for g in range(GROUPS):
        y_share(g).start()
        own_share(g).start()

    @pl.loop(0, DEPTH)
    def _(i):
        out_batch(i)

    @pl.when(p == 0)
    def _():
        band[0] = jnp.zeros_like(band[0])

    @pl.loop(0, GROUPS)
    def _(g):
        own_share(g).wait()
        y_share(g).wait_recv()
        plus(g, 0, z).start()
        minus(g, 0, z).start()
        across(g, 0, z).start()

    for r in (0, 2):
        when(jnp.logical_not(in_band(r, p)), lambda r=r: rest_copy(r).start())

    for j in range(4):
        @pl.loop(0, GROUPS)
        def _(g, j=j):
            event = j * GROUPS + g
            plus(g, j, (z + 7 - j) % 8).wait_recv()
            if j < 3:
                plus(g, j + 1, (z + 7 - j) % 8).start()
                across(g, 1 + j, block_z[1 + j]).start()
            minus(g, j, (z + 1 + j) % 8).wait_recv()
            if j < 3:
                minus(g, j + 1, (z + 1 + j) % 8).start()
                across(g, 4 + j, block_z[4 + j]).start()
            else:
                across(g, 7, block_z[7]).start()

            @pl.when(jnp.logical_and(event % 2 == 0, event < 2 * (3 * HELD - DEPTH)))
            def _():
                out_batch(DEPTH + event // 2)

            if j == 3:
                theirs = qf.at[pl.ds(2 * g, 2), :, 1 - core]
                remote(theirs, theirs, c_s.at[0], c_r.at[g], dsts[0], q).wait_recv()

                @pl.when(g == 0)
                def _():
                    when(mine, lambda: right_own().wait())

                    when(mine, lambda: right_received(SPAN - 1))
                    when(jnp.logical_not(mine), lambda: right_received(SPAN))

                @pl.loop(2 * g, 2 * g + 2)
                def _(w):
                    convert(w)
                    right_window(w)

    @pl.loop(1, COLP)
    def _(u):
        when(col_in((q + u) % COLP), lambda: right_back(u).start())

    when(mine, lambda: right_back_own().start())
    needs = [[w for w in range(WINS) if (first + 2 * w + 3) // 8 >= r][0] for r in range(3)]

    @pl.loop(0, WINS)
    def _(w):
        @pl.when(w == needs[0])
        def _():
            out_wait(0)

        @pl.when(w == needs[1])
        def _():
            out_wait(1)

        @pl.when(w == needs[2])
        def _():
            when(mine, lambda: right_back_own().wait())
            when(jnp.logical_not(mine), lambda: cols_plain().wait())

            ref = cbuf.at[:, pl.ds(0, 4 * (COLP - 1))]
            when(mine, lambda: remote(ref, ref, rt_s.at[1], rt_r.at[0], dsts[0], q).wait_recv())

            for r in range(3):
                when(both(in_band(r, p), p != 0), lambda r=r: first_out(r).start())
                when(both(in_band(r, p), p == 0), lambda r=r: first_own(r).start())
                if r != 1:
                    when(jnp.logical_not(in_band(r, p)), lambda r=r: rest_first(r).start())
            out_wait(2)

        @pl.loop(0, 2)
        def _(pr):
            left_window(w, pr * 2, 2)

        @pl.when(w % 2 == 1)
        def _():
            @pl.when(w == 3)
            def _():
                back_send(0)

            @pl.when(w == 7)
            def _():
                back_send(1)

            @pl.when(w == 9)
            def _():
                back_send(2)

    @pl.when(p == 0)
    def _():
        for r in range(3):
            when(in_band(r, p), lambda r=r: first_own(r).wait())
            for s in range(1, 8):
                if in_band(r, s):
                    first_in(r, s).wait_recv()

        @pl.loop(0, WINS)
        def _(w):
            left_window(w, HELD, 1)

        for r in range(3):
            when(in_band(r, p), lambda r=r: first_back_own(r).start())
            for s in range(1, 8):
                if in_band(r, s):
                    first_back(r, s).start()

    def right_returned(count):
        ref = rbuf.at[pl.ds(0, count), pl.ds(0, 3)]
        remote(ref, ref, rt_s.at[1], rt_r.at[0], dsts[0], q).wait_send()

    sent = cbuf.at[:, pl.ds(0, 4 * (COLP - 1))]
    when(mine, lambda: remote(sent, sent, rr_s.at[1], rr_r.at[0], dsts[0], q).wait_send())
    when(mine, lambda: right_returned(SPAN - 1))
    when(jnp.logical_not(mine), lambda: right_returned(SPAN))

    for ref, sem, got in (
        (qf.at[:, z, core, yl], y_s, y_r),
        (qf.at[pl.ds(0, GROUPS), pl.ds(0, 7), core], zp_s, c_r),
        (qf.at[pl.ds(0, GROUPS), pl.ds(0, 7), core], zm_s, c_r),
        (qf.at[:, :, core], c_s, c_r),
    ):
        remote(ref, ref, sem.at[0], got.at[0], dsts[0], q).wait_send()

    @pl.loop(3 * HELD - DEPTH, 3 * HELD)
    def _(i):
        out_sent(i)

    for r in range(3):
        back_wait(r)
        when(both(in_band(r, p), p != 0), lambda r=r: first_out(r).wait_send())
        when(both(in_band(r, p), p != 0), lambda r=r: first_back(r, p).wait_recv())
        if r != 1:
            when(jnp.logical_not(in_band(r, p)), lambda r=r: rest_copy(r).wait())
            when(jnp.logical_not(in_band(r, p)), lambda r=r: rest_first(r).wait())

    @pl.when(p == 0)
    def _():
        for r in range(3):
            when(in_band(r, p), lambda r=r: first_back_own(r).wait())
            for s in range(1, 8):
                if in_band(r, s):
                    first_back(r, s).wait_send()


def update(first, tiles, shares):
    dma = pltpu.SemaphoreType.DMA
    return pl.pallas_call(
        functools.partial(kernel, first),
        out_shape=jax.ShapeDtypeStruct(tiles.shape, tiles.dtype),
        in_specs=[pl.BlockSpec(memory_space=pl.ANY)] * 2,
        out_specs=pl.BlockSpec(memory_space=pl.ANY),
        scratch_shapes=[
            pltpu.VMEM((HELD + 1, 24 * NB, NB), jnp.float32),
            pltpu.VMEM((WINS, 8, 2, 2, 16, WIN), jnp.float32),
            pltpu.VMEM((WINS, WIN, WIN), jnp.bfloat16),
            pltpu.VMEM((WINS, WIN, WIN), jnp.bfloat16),
            pltpu.VMEM((WIN, 2 * NB), jnp.bfloat16),
            pltpu.VMEM((WIN, 2 * NB), jnp.bfloat16),
            pltpu.VMEM((24, 4, 4, NB), jnp.float32),
            pltpu.VMEM((3, NB, 1, NB), jnp.float32),
            dma((3, HELD)), dma((3,)), dma((3,)), dma((3,)), dma((3,)), dma((3,)), dma((3, 2)),
            dma((GROUPS,)), dma((1,)), dma((GROUPS,)),
            dma((1,)), dma((GROUPS, 4)), dma((1,)), dma((GROUPS, 4)),
            dma((1,)), dma((GROUPS,)),
            dma((2,)), dma((1,)), dma((2,)), dma((1,)),
            dma((3,)), dma((3, ROWP)), dma((3, ROWP)), dma((3,)),
        ],
        compiler_params=pltpu.CompilerParams(
            collective_id=first, has_side_effects=True, vmem_limit_bytes=50 * 2**20
        ),
        cost_estimate=pl.CostEstimate(flops=8 * 10**9, bytes_accessed=20 * 10**6, transcendentals=0),
        name=f"sweep{first}",
    )(tiles, shares)


def body(matrix, factors, starts):
    tiles = matrix.reshape(3, NB, COLP, 1, NB)
    shares = jnp.transpose(factors, (0, 2, 1))
    updated = lax.switch(
        starts[0] // NB, [functools.partial(update, first) for first in range(3)], tiles, shares
    )
    return updated.reshape(matrix.shape)


def solution(mesh):
    placed = (P(None, "row", None, None, "col", None), P(None, None, "col"), P())
    return jax.shard_map(
        body,
        mesh=mesh,
        in_specs=placed,
        out_specs=P(None, "row", None, None, "col", None),
        check_vma=False,
    )
```

```python
import functools

import jax
import jax.numpy as jnp
from jax import lax
from jax.experimental import pallas as pl
from jax.experimental.pallas import tpu as pltpu
from jax.sharding import PartitionSpec as P

MESH = pl.DeviceIdType.MESH
NB = 128
WIN = 512
WINS = 10
SPAN = 22
GROUPS = 5
ROWP = 8
COLP = 32
HELD = 4
DEPTH = 2
PEERS = ((0, 1), (1, 0), (2, 1), (3, 0), (1, 1), (2, 0), (3, 1))


def when(condition, action):
    if isinstance(condition, bool):
        if condition:
            action()
    else:
        pl.when(condition)(action)


def both(*conditions):
    result = True
    for condition in conditions:
        if condition is True:
            continue
        if condition is False:
            return False
        result = condition if result is True else jnp.logical_and(result, condition)
    return result


def split(value):
    high = value.astype(jnp.bfloat16)
    low = (value - high.astype(jnp.float32)).astype(jnp.bfloat16)
    return high, low


def dot(a, b):
    return jnp.dot(a, b, preferred_element_type=jnp.float32)


def dot_t(a, b):
    return lax.dot_general(a, b, (((1,), (1,)), ((), ())), preferred_element_type=jnp.float32)


def kernel(first, m, qt, o, band, qf, qh, ql, xh, xl, rbuf, cbuf,
           out_s, out_r, back_s, back_r, own_s, bown_s, rest_s,
           loc_s, y_s, y_r, zp_s, zp_r, zm_s, zm_r, c_s, c_r,
           rr_s, rr_r, rt_s, rt_r, c0_s, c0_r, cb_s, cb_r):
    p = lax.axis_index("row")
    q = lax.axis_index("col")
    x, yh = p // 2, p % 2
    z, yl, core = q // 4, (q // 2) % 2, q % 2

    dsts = [((x + dx) % 4) * 2 + (yh + dy) % 2 for dx, dy in PEERS]
    srcs = [((x + 4 - dx) % 4) * 2 + (yh + dy) % 2 for dx, dy in PEERS]

    def remote(src, dst, ss, rs, row, col):
        return pltpu.make_async_remote_copy(
            src, dst, ss, rs, device_id={"row": row, "col": col}, device_id_type=MESH
        )

    def local(src, dst, s):
        return pltpu.make_async_copy(src, dst, s)

    def in_band(r, s):
        tile = r * 8 + s
        if isinstance(tile, int):
            return first <= tile < first + SPAN
        if isinstance(r, int):
            return True if r == 1 else tile >= first if r == 0 else tile < first + SPAN
        return jnp.logical_and(tile >= first, tile < first + SPAN)

    def rows(tile):
        return pl.ds(pl.multiple_of(tile * NB, NB), NB)

    barrier = pltpu.get_barrier_semaphore()
    for d in dsts:
        pl.semaphore_signal(barrier, inc=1, device_id={"row": d, "col": q}, device_id_type=MESH)

    @pl.loop(1, COLP)
    def _(u):
        pl.semaphore_signal(
            barrier, inc=1, device_id={"row": p, "col": (q + u) % COLP}, device_id_type=MESH
        )

    pl.semaphore_wait(barrier, len(PEERS) + COLP - 1)

    mine = jnp.logical_and(q >= first, q < first + SPAN)

    def col_in(s):
        return jnp.logical_and(s >= first, s < first + SPAN)

    def right_send(u):
        to = (q + u) % COLP
        return remote(
            m.at[:, pl.ds(4 * to, 4), 0, 0], rbuf.at[q, pl.ds(0, 3)], rr_s.at[1], rr_r.at[0], p, to
        )

    def right_own():
        return local(m.at[:, pl.ds(4 * q, 4), 0, 0], rbuf.at[q, pl.ds(0, 3)], rr_s.at[0])

    def right_received(count):
        ref = rbuf.at[pl.ds(0, count), pl.ds(0, 3)]
        remote(ref, ref, rr_s.at[1], rr_r.at[0], dsts[0], q).wait_recv()

    def right_back(u):
        to = (q + u) % COLP
        return remote(
            rbuf.at[to, pl.ds(0, 3)], cbuf.at[:, pl.ds(4 * q, 4), 0], rt_s.at[1], rt_r.at[0], p, to
        )

    def right_back_own():
        return local(rbuf.at[q, pl.ds(0, 3)], cbuf.at[:, pl.ds(4 * q, 4), 0], rt_s.at[0])

    def cols_plain():
        return local(m.at[:, :, 0], cbuf, rt_s.at[0])

    def pair(g, zz, which, n=2, at=0):
        return qf.at[pl.ds(2 * g + at, n), zz, which]

    def own_share(g):
        return local(qt.at[pl.ds(2 * g, 2)], qf.at[pl.ds(2 * g, 2), z, core, yl], loc_s.at[g])

    def y_share(g):
        return remote(
            qt.at[pl.ds(2 * g, 2)], qf.at[pl.ds(2 * g, 2), z, core, yl], y_s.at[0], y_r.at[g],
            p, z * 4 + (1 - yl) * 2 + core,
        )

    def plus(g, j, zz):
        ref = pair(g, zz, core) if j < 3 else pair(g, zz, core, 1, 0)
        return remote(ref, ref, zp_s.at[0], zp_r.at[g, j], p, ((z + 1) % 8) * 4 + yl * 2 + core)

    def minus(g, j, zz):
        ref = pair(g, zz, core) if j < 3 else pair(g, zz, core, 1, 1)
        return remote(ref, ref, zm_s.at[0], zm_r.at[g, j], p, ((z + 7) % 8) * 4 + yl * 2 + core)

    def across(g, b, zz):
        ref = pair(g, zz, core)
        return remote(ref, ref, c_s.at[0], c_r.at[g], p, z * 4 + yl * 2 + 1 - core)

    block_z = [z, (z + 7) % 8, (z + 6) % 8, (z + 5) % 8, (z + 1) % 8, (z + 2) % 8, (z + 3) % 8, (z + 4) % 8]

    def out_copy(r, h, k):
        d = dsts[k]
        return remote(
            m.at[r, :, 4 * d + h, 0], band.at[h, rows(r * 8 + p)], out_s.at[r, h], out_r.at[r], d, q
        )

    def own_copy(r, h):
        return local(m.at[r, :, 4 * p + h, 0], band.at[h, rows(r * 8 + p)], own_s.at[r])

    def held(h, who):
        return jnp.logical_not(jnp.logical_and(h == 0, who == 0))

    def out_batch(i):
        r, h = i // HELD, i % HELD

        @pl.when(i >= DEPTH)
        def _():
            out_sent(i - DEPTH)

        for k, d in enumerate(dsts):
            when(both(in_band(r, p), held(h, d)), lambda k=k: out_copy(r, h, k).start())
        when(both(in_band(r, p), held(h, p)), lambda: own_copy(r, h).start())

    def tiles_ref(slots, count):
        return band.at[pl.ds(0, slots), pl.ds(0, count * NB)]

    def await_sent(slots, count, sem):
        ref = tiles_ref(slots, count)
        remote(ref, ref, sem, out_r.at[0], dsts[0], q).wait_send()

    def await_received(slots, count, sem):
        ref = tiles_ref(slots, count)
        remote(ref, ref, out_s.at[0, 0], sem, dsts[0], q).wait_recv()

    def per_peer(r, action):
        valid = sum(in_band(r, s) for s in range(8))
        for slots, which in ((HELD, p != 0), (HELD - 1, p == 0)):
            when(both(which, in_band(r, p)), lambda slots=slots: action(slots, valid - 1))
            if r != 1:
                when(
                    both(which, jnp.logical_not(in_band(r, p))),
                    lambda slots=slots: action(slots, valid),
                )

    def own_wait(r, sem):
        for slots, which in ((HELD, p != 0), (HELD - 1, p == 0)):
            ref = tiles_ref(slots, 1)
            when(both(which, in_band(r, p)), lambda ref=ref: local(ref, ref, sem).wait())

    def out_wait(r):
        per_peer(r, lambda slots, count: await_received(slots, count, out_r.at[r]))
        own_wait(r, own_s.at[r])

    def out_sent(i):
        r, h = i // HELD, i % HELD
        fewer = jnp.logical_and(h == 0, p != 0)
        when(both(in_band(r, p), fewer), lambda: await_sent(1, 6, out_s.at[r, h]))
        when(both(in_band(r, p), jnp.logical_not(fewer)), lambda: await_sent(1, 7, out_s.at[r, h]))

    def back_copy(r, h, k):
        d = dsts[k]
        return remote(
            band.at[h, rows(r * 8 + d)], o.at[r, :, 4 * p + h, 0], back_s.at[r], back_r.at[r], d, q
        )

    def back_own(r, h):
        return local(band.at[h, rows(r * 8 + p)], o.at[r, :, 4 * p + h, 0], bown_s.at[r])

    def back_send(r):
        @pl.loop(0, HELD)
        def _(h):
            for k, d in enumerate(dsts):
                when(both(in_band(r, d), held(h, p)), lambda k=k: back_copy(r, h, k).start())
            when(both(in_band(r, p), held(h, p)), lambda: back_own(r, h).start())

    def back_wait(r):
        per_peer(r, lambda slots, count: await_sent(slots, count, back_s.at[r]))
        own_wait(r, bown_s.at[r])
        when(both(in_band(r, p), p == 0), lambda: await_received(4, 7, back_r.at[r]))
        when(both(in_band(r, p), p != 0), lambda: await_received(3, 9, back_r.at[r]))

    def rest_copy(r):
        return local(m.at[r, :, pl.ds(1, 31)], o.at[r, :, pl.ds(1, 31)], rest_s.at[r, 0])

    def rest_first(r):
        return local(cbuf.at[r], o.at[r, :, 0], rest_s.at[r, 1])

    def first_out(r):
        return remote(cbuf.at[r, :, 0], band.at[HELD, rows(r * 8 + p)], c0_s.at[r], c0_r.at[r, p], 0, q)

    def first_in(r, s):
        return remote(cbuf.at[r, :, 0], band.at[HELD, rows(r * 8 + s)], c0_s.at[r], c0_r.at[r, s], 0, q)

    def first_own(r):
        return local(cbuf.at[r, :, 0], band.at[HELD, rows(r * 8)], c0_s.at[r])

    def first_back(r, s):
        return remote(band.at[HELD, rows(r * 8 + s)], o.at[r, :, 0, 0], cb_s.at[r, s], cb_r.at[r], s, q)

    def first_back_own(r):
        return local(band.at[HELD, rows(r * 8)], o.at[r, :, 0, 0], cb_s.at[r, 0])

    def convert(w):
        @pl.loop(0, 8)
        def _(zz):
            for a in range(2):
                for b in range(2):
                    at = pl.ds(pl.multiple_of(zz * 64 + b * 32 + a * 16, 16), 16)
                    high, low = split(qf[w, zz, a, b])
                    qh[w, at, :] = high
                    ql[w, at, :] = low

    def left_window(w, h, n):
        base = (first + 2 * w) * NB
        for i in range(n):
            high, low = split(band[h + i, pl.ds(pl.multiple_of(base, NB), WIN), :])
            xh[:, i * NB:(i + 1) * NB] = high
            xl[:, i * NB:(i + 1) * NB] = low
        xhv, xlv = xh[:, : n * NB], xl[:, : n * NB]

        @pl.loop(0, 2)
        def _(part):
            at = pl.ds(pl.multiple_of(part * 256, 256), 256)
            qhv, qlv = qh[w, at, :], ql[w, at, :]
            y = dot(qhv, xhv) + dot(qhv, xlv) + dot(qlv, xhv)
            to = pl.ds(pl.multiple_of(base + part * 256, NB), 256)
            for i in range(n):
                band[h + i, to, :] = y[:, i * NB:(i + 1) * NB]

    flat = rbuf.reshape(24 * 16, NB)

    def right_window(w):
        ats = [pl.ds(pl.multiple_of((first + 2 * w + j) * 16, 16), 16) for j in range(4)]
        value = jnp.concatenate([flat[at, :] for at in ats], axis=1)
        high, low = split(value)
        qhv, qlv = qh[w], ql[w]
        y = dot_t(high, qhv) + dot_t(low, qhv) + dot_t(high, qlv)
        for j, at in enumerate(ats):
            flat[at, :] = y[:, j * NB:(j + 1) * NB]

    for g in range(GROUPS):
        y_share(g).start()
        own_share(g).start()

    @pl.loop(0, DEPTH)
    def _(i):
        out_batch(i)

    @pl.when(p == 0)
    def _():
        band[0] = jnp.zeros_like(band[0])

    @pl.loop(0, GROUPS)
    def _(g):
        own_share(g).wait()
        y_share(g).wait_recv()
        plus(g, 0, z).start()
        minus(g, 0, z).start()
        across(g, 0, z).start()

    when(mine, lambda: right_own().start())

    @pl.when(mine)
    def _():
        @pl.loop(1, COLP)
        def _(u):
            right_send(u).start()

    when(jnp.logical_not(mine), lambda: cols_plain().start())

    for r in (0, 2):
        when(jnp.logical_not(in_band(r, p)), lambda r=r: rest_copy(r).start())

    for j in range(4):
        @pl.loop(0, GROUPS)
        def _(g, j=j):
            event = j * GROUPS + g
            plus(g, j, (z + 7 - j) % 8).wait_recv()
            if j < 3:
                plus(g, j + 1, (z + 7 - j) % 8).start()
                across(g, 1 + j, block_z[1 + j]).start()
            minus(g, j, (z + 1 + j) % 8).wait_recv()
            if j < 3:
                minus(g, j + 1, (z + 1 + j) % 8).start()
                across(g, 4 + j, block_z[4 + j]).start()
            else:
                across(g, 7, block_z[7]).start()

            @pl.when(jnp.logical_and(event % 2 == 0, event < 2 * (3 * HELD - DEPTH)))
            def _():
                out_batch(DEPTH + event // 2)

            if j == 3:
                theirs = qf.at[pl.ds(2 * g, 2), :, 1 - core]
                remote(theirs, theirs, c_s.at[0], c_r.at[g], dsts[0], q).wait_recv()

                @pl.when(g == 0)
                def _():
                    when(mine, lambda: right_own().wait())

                    when(mine, lambda: right_received(SPAN - 1))
                    when(jnp.logical_not(mine), lambda: right_received(SPAN))

                @pl.loop(2 * g, 2 * g + 2)
                def _(w):
                    convert(w)
                    right_window(w)

    @pl.loop(1, COLP)
    def _(u):
        when(col_in((q + u) % COLP), lambda: right_back(u).start())

    when(mine, lambda: right_back_own().start())
    needs = [[w for w in range(WINS) if (first + 2 * w + 3) // 8 >= r][0] for r in range(3)]

    @pl.loop(0, WINS)
    def _(w):
        @pl.when(w == needs[0])
        def _():
            out_wait(0)

        @pl.when(w == needs[1])
        def _():
            out_wait(1)

        @pl.when(w == needs[2])
        def _():
            when(mine, lambda: right_back_own().wait())
            when(jnp.logical_not(mine), lambda: cols_plain().wait())

            ref = cbuf.at[:, pl.ds(0, 4 * (COLP - 1))]
            when(mine, lambda: remote(ref, ref, rt_s.at[1], rt_r.at[0], dsts[0], q).wait_recv())

            for r in range(3):
                when(both(in_band(r, p), p != 0), lambda r=r: first_out(r).start())
                when(both(in_band(r, p), p == 0), lambda r=r: first_own(r).start())
                if r != 1:
                    when(jnp.logical_not(in_band(r, p)), lambda r=r: rest_first(r).start())
            out_wait(2)

        @pl.loop(0, 2)
        def _(pr):
            left_window(w, pr * 2, 2)

        @pl.when(w % 2 == 1)
        def _():
            @pl.when(w == 3)
            def _():
                back_send(0)

            @pl.when(w == 7)
            def _():
                back_send(1)

            @pl.when(w == 9)
            def _():
                back_send(2)

    @pl.when(p == 0)
    def _():
        for r in range(3):
            when(in_band(r, p), lambda r=r: first_own(r).wait())
            for s in range(1, 8):
                if in_band(r, s):
                    first_in(r, s).wait_recv()

        @pl.loop(0, WINS)
        def _(w):
            left_window(w, HELD, 1)

        for r in range(3):
            when(in_band(r, p), lambda r=r: first_back_own(r).start())
            for s in range(1, 8):
                if in_band(r, s):
                    first_back(r, s).start()

    def right_returned(count):
        ref = rbuf.at[pl.ds(0, count), pl.ds(0, 3)]
        remote(ref, ref, rt_s.at[1], rt_r.at[0], dsts[0], q).wait_send()

    sent = cbuf.at[:, pl.ds(0, 4 * (COLP - 1))]
    when(mine, lambda: remote(sent, sent, rr_s.at[1], rr_r.at[0], dsts[0], q).wait_send())
    when(mine, lambda: right_returned(SPAN - 1))
    when(jnp.logical_not(mine), lambda: right_returned(SPAN))

    for ref, sem, got in (
        (qf.at[:, z, core, yl], y_s, y_r),
        (qf.at[pl.ds(0, GROUPS), pl.ds(0, 7), core], zp_s, c_r),
        (qf.at[pl.ds(0, GROUPS), pl.ds(0, 7), core], zm_s, c_r),
        (qf.at[:, :, core], c_s, c_r),
    ):
        remote(ref, ref, sem.at[0], got.at[0], dsts[0], q).wait_send()

    @pl.loop(3 * HELD - DEPTH, 3 * HELD)
    def _(i):
        out_sent(i)

    for r in range(3):
        back_wait(r)
        when(both(in_band(r, p), p != 0), lambda r=r: first_out(r).wait_send())
        when(both(in_band(r, p), p != 0), lambda r=r: first_back(r, p).wait_recv())
        if r != 1:
            when(jnp.logical_not(in_band(r, p)), lambda r=r: rest_copy(r).wait())
            when(jnp.logical_not(in_band(r, p)), lambda r=r: rest_first(r).wait())

    @pl.when(p == 0)
    def _():
        for r in range(3):
            when(in_band(r, p), lambda r=r: first_back_own(r).wait())
            for s in range(1, 8):
                if in_band(r, s):
                    first_back(r, s).wait_send()


def update(first, tiles, shares):
    dma = pltpu.SemaphoreType.DMA
    return pl.pallas_call(
        functools.partial(kernel, first),
        out_shape=jax.ShapeDtypeStruct(tiles.shape, tiles.dtype),
        in_specs=[pl.BlockSpec(memory_space=pl.ANY)] * 2,
        out_specs=pl.BlockSpec(memory_space=pl.ANY),
        scratch_shapes=[
            pltpu.VMEM((HELD + 1, 24 * NB, NB), jnp.float32),
            pltpu.VMEM((WINS, 8, 2, 2, 16, WIN), jnp.float32),
            pltpu.VMEM((WINS, WIN, WIN), jnp.bfloat16),
            pltpu.VMEM((WINS, WIN, WIN), jnp.bfloat16),
            pltpu.VMEM((WIN, 2 * NB), jnp.bfloat16),
            pltpu.VMEM((WIN, 2 * NB), jnp.bfloat16),
            pltpu.VMEM((24, 4, 4, NB), jnp.float32),
            pltpu.VMEM((3, NB, 1, NB), jnp.float32),
            dma((3, HELD)), dma((3,)), dma((3,)), dma((3,)), dma((3,)), dma((3,)), dma((3, 2)),
            dma((GROUPS,)), dma((1,)), dma((GROUPS,)),
            dma((1,)), dma((GROUPS, 4)), dma((1,)), dma((GROUPS, 4)),
            dma((1,)), dma((GROUPS,)),
            dma((2,)), dma((1,)), dma((2,)), dma((1,)),
            dma((3,)), dma((3, ROWP)), dma((3, ROWP)), dma((3,)),
        ],
        compiler_params=pltpu.CompilerParams(
            collective_id=first, has_side_effects=True, vmem_limit_bytes=50 * 2**20
        ),
        cost_estimate=pl.CostEstimate(flops=8 * 10**9, bytes_accessed=20 * 10**6, transcendentals=0),
        name=f"sweep{first}",
    )(tiles, shares)


def body(matrix, factors, starts):
    tiles = matrix.reshape(3, NB, COLP, 1, NB)
    shares = jnp.transpose(factors, (0, 2, 1))
    updated = lax.switch(
        starts[0] // NB, [functools.partial(update, first) for first in range(3)], tiles, shares
    )
    return updated.reshape(matrix.shape)


def solution(mesh):
    placed = (P(None, "row", None, None, "col", None), P(None, None, "col"), P())
    return jax.shard_map(
        body,
        mesh=mesh,
        in_specs=placed,
        out_specs=P(None, "row", None, None, "col", None),
        check_vma=False,
    )
```
